128 devices in a mesh: patch: 64 (over x, z, y_lo, core), head: 2 (over y_hi).
Axes of the slice: x: 4, y: 4 (y_hi: 2, y_lo: 2; y = y_hi * 2 + y_lo), z: 4, core: 2. Of those that a mesh axis runs over, the one named last changes fastest.
Arguments:
- hidden: bfloat16 [2, 12288, 3072], P(None, ('patch', 'head')), may hold values from -2.5 to 2.5
- queries: bfloat16 [2, 12288, 1536], P(None, ('patch', 'head')), may hold values from -8 to 8
- keys: bfloat16 [2, 12288, 1536], P(None, ('patch', 'head')), may hold values from -8 to 8
- values: bfloat16 [2, 12288, 1536], P(None, ('patch', 'head')), may hold values from -6 to 6
- out_weight: bfloat16 [1536, 3072], replicated, may hold values from -0.15625 to 0.15625
- gate_table: float32 [50, 3072], replicated, may hold values from -4 to 4
- steps_t: int32 [2], replicated, may hold values from 0 to 49
Outputs:
- blocked: bfloat16 [2, 12288, 3072], P(None, ('patch', 'head'))
The draws below stay inside these ranges and needn't reach their ends.
All inputs are finite; a program needn't handle non-finite values.
Results may differ from the reference program's by a relative error of at most 0.008.
Values may be sent and summed in bfloat16 or wider, within the bound.
A program may use at most 192 MiB of HBM per device.

```python
import math
import jax
import jax.numpy as jnp
from jax import lax

D = 3072
HEADS = 12
HD = 128
NUM_T = 50
STEPS = 2
TOK_DEV = 96
TOKENS = 12288
N_PATCH = 64
N_HEAD = 2


def draw_queries(key, part):
    key = jax.random.fold_in(key, 11)
    result = 1.6 * jnp.clip(jax.random.normal(key, (STEPS, TOKENS, HEADS * HD), jnp.float32), -5.0, 5.0)
    return result.astype(jnp.bfloat16)


def draw_keys(key, part):
    key = jax.random.fold_in(key, 12)
    result = 1.6 * jnp.clip(jax.random.normal(key, (STEPS, TOKENS, HEADS * HD), jnp.float32), -5.0, 5.0)
    return result.astype(jnp.bfloat16)


def shard_levels(own_key, dims, pieces, smallest, high):
    factor_of = 1.0
    for axis_at, parts in pieces:
        draws = jax.random.uniform(jax.random.fold_in(jax.random.fold_in(own_key, 6), axis_at), (parts,), jnp.float32, smallest / len(pieces), high / len(pieces))
        factor_of = factor_of * jnp.repeat(jnp.exp(draws), dims[axis_at] // parts).reshape((-1,) + (1,) * (len(dims) - 1 - axis_at))
    return factor_of


def bell_draw(rng, dims, scale, limit, shards=(), kind=jnp.bfloat16):
    level = shard_levels(rng, dims, shards, -0.22, 0.18) if shards else 1.0
    array = jax.random.normal(rng, dims, jnp.float32) * scale * level
    return jnp.minimum(jnp.maximum(array, -limit), limit).astype(kind)


def setup_inputs(seed: int = 0) -> dict:
    key_list = jax.random.split(jax.random.key(seed), 8)
    return {
        "hidden": bell_draw(key_list[0], (STEPS, TOKENS, D), 0.25, 2.5, ((1, 128),)),
        "queries": draw_queries(jax.random.fold_in(key_list[7], 71), 0),
        "keys": draw_keys(jax.random.fold_in(key_list[7], 71), 0),
        "values": bell_draw(key_list[3], (STEPS, TOKENS, HEADS * HD), 1.0, 6.0, ((1, 128),)),
        "out_weight": bell_draw(key_list[4], (HEADS * HD, D), (HEADS * HD) ** -0.5, 0.15625),
        "gate_table": bell_draw(key_list[5], (NUM_T, D), 1.0, 4.0, (), jnp.float32),
        "steps_t": jax.random.randint(key_list[6], (STEPS,), 0, NUM_T).astype(jnp.int32),
    }


def attend_group(query_rows, key_table, value_table):
    group_rows = query_rows.shape[0]
    total_rows = key_table.shape[0]
    query_heads = query_rows.astype(jnp.float32).reshape(group_rows, HEADS, HD)
    key_heads = key_table.astype(jnp.float32).reshape(total_rows, HEADS, HD)
    value_heads = value_table.astype(jnp.float32).reshape(total_rows, HEADS, HD)
    scores = jnp.einsum('qhd,khd->hqk', query_heads, key_heads) * (1.0 / math.sqrt(HD))
    top_score = lax.optimization_barrier(jnp.max(scores, axis=-1, keepdims=True))
    lifted = jnp.exp(scores - top_score)
    weight_sum = lax.optimization_barrier(jnp.sum(lifted, axis=-1))
    lowered = lax.optimization_barrier(lifted.astype(jnp.bfloat16)).astype(jnp.float32)
    weighted = jnp.einsum('hqk,khd->hqd', lowered, value_heads)
    result = weighted / weight_sum[:, :, None]
    return jnp.transpose(result, (1, 0, 2)).reshape(group_rows, HEADS * HD).astype(jnp.bfloat16)

def reference(hidden, queries, keys, values, out_weight, gate_table, steps_t):
    group_rows = TOK_DEV * N_HEAD
    starts = jnp.arange(N_PATCH, dtype=jnp.int32) * group_rows

    def first_group(offset):
        query_rows = lax.dynamic_slice_in_dim(queries[0], offset, group_rows, 0)
        return attend_group(query_rows, keys[0], values[0])

    def second_group(offset):
        query_rows = lax.dynamic_slice_in_dim(queries[1], offset, group_rows, 0)
        key_table = lax.dynamic_update_slice_in_dim(keys[0], lax.dynamic_slice_in_dim(keys[1], offset, group_rows, 0), offset, 0)
        value_table = lax.dynamic_update_slice_in_dim(values[0], lax.dynamic_slice_in_dim(values[1], offset, group_rows, 0), offset, 0)
        return attend_group(query_rows, key_table, value_table)
    first = lax.map(first_group, starts).reshape(TOKENS, HEADS * HD)
    second = lax.map(second_group, starts).reshape(TOKENS, HEADS * HD)
    gate_rows = gate_table[steps_t]
    outputs = []
    for step_id, attended in enumerate((first, second)):
        projected = jnp.dot(attended, out_weight, preferred_element_type=jnp.float32)
        outputs.append((hidden[step_id].astype(jnp.float32) + gate_rows[step_id][None, :] * projected).astype(jnp.bfloat16))
    return jnp.stack(outputs)
```

```python
import functools
import math

import jax
import jax.numpy as jnp
from jax import lax
from jax.experimental import pallas as pl
from jax.experimental.pallas import tpu as pltpu
from jax.sharding import PartitionSpec as P

HD = 128
TOK = 96
CHUNK = 4 * TOK
QUERIES = 2 * CHUNK
RING = 4
SLOTS = 3
TILE = 256
LOG2_SCALE = math.log2(math.e) / math.sqrt(HD)
LOWEST = -1e30

SPREAD = ("y", "x", "z")
PLANE = (("x", "z"), ("y", "z"), ("y", "x"))

VISITS = (
    (1, 0), (3, 0), (0, 1), (0, 3), (1, 1), (3, 3), (1, 3), (3, 1),
    (0, 2), (2, 1), (1, 2), (2, 3), (3, 2), (2, 2),
)
PARTNER = (2, 0)

ARRIVALS = {
    0: ((1, 0), (0, 1)),
    1: ((3, 0), (0, 3)),
    2: ((2, 0), (1, 1), (1, 3)),
    3: ((3, 1), (3, 3)),
    4: ((0, 2),),
    5: ((2, 1), (2, 3)),
    7: ((1, 2), (3, 2)),
    9: ((2, 2),),
}


def block_of(index):
    return sum((index >= edge * TOK).astype(jnp.int32) for edge in range(1, RING))


def kernel(
    hidden, queries, keys, values, weight, gates, steps, out,
    kv, kv1, v_in, v1_in, q_in, qt, acc, top, total, o_out, att, w_buf, g_buf, h_buf,
    ex_send, ex_recv, ag_send, ag_recv, sib_recv, ret_send, ret_recv, local,
):
    patch, head = lax.axis_index("patch"), lax.axis_index("head")
    core = lax.rem(patch, 2)
    at = {
        "x": patch // 16,
        "z": lax.rem(patch // 4, RING),
        "y": head * 2 + lax.rem(patch // 2, 2),
    }

    def device(**moved):
        pos = dict(at, core=core)
        pos.update(moved)
        y = pos["y"]
        return (((pos["x"] * RING + pos["z"]) * 2 + lax.rem(y, 2)) * 2 + pos["core"], y // 2)

    def shifted(axis, step):
        return lax.rem(at[axis] + step, RING)

    def pick(first, second):
        return first + core * (second - first)

    def routed(s, which, step):
        a, b = PLANE[s] if which == 0 else PLANE[s][::-1]
        da, db = device(**{a: shifted(a, step)}), device(**{b: shifted(b, step)})
        return (pick(da[0], db[0]), pick(da[1], db[1]))

    def chip_at(s, da, db):
        a, b = PLANE[s]
        return shifted(a, da) * RING + shifted(b, db)

    def chip_routed(s, first, second):
        return pick(chip_at(s, first, second), chip_at(s, second, first))

    sibling = device(core=1 - core)
    far_y = shifted("y", 2)

    peers = [device(**{axis: shifted(axis, step)}) for axis in "xyz" for step in (1, 2, 3)]
    peers += [device(y=far_y, **{axis: shifted(axis, step)}) for axis in "xz" for step in (1, 2, 3)]
    peers.append(sibling)
    barrier = pltpu.get_barrier_semaphore()
    for peer in peers:
        pl.semaphore_signal(barrier, inc=1, device_id=peer, device_id_type=pl.DeviceIdType.MESH)
    pl.semaphore_wait(barrier, len(peers))

    sent, gathered = [], []

    def remote(src, dst, send_sem, recv_sem, target, start=True):
        copy = pltpu.make_async_remote_copy(
            src_ref=src, dst_ref=dst, send_sem=send_sem, recv_sem=recv_sem,
            device_id=target, device_id_type=pl.DeviceIdType.MESH,
        )
        if start:
            copy.start()
        return copy

    def rows_of(place):
        return pl.ds(pl.multiple_of(place * TOK, TOK), TOK)

    def columns_of(place):
        return pl.ds(pl.multiple_of(place * HD, HD), HD)

    def own_chip(s):
        return chip_at(s, 0, 0)

    def pieces(s, target_place, source_place):
        cols = columns_of(4 * s + target_place)
        rows = rows_of(source_place)
        return (
            (keys.at[0, :, cols], kv.at[s, own_chip(s), core, 0, rows, :]),
            (values.at[0, :, cols], v_in.at[s, rows, :]),
            (queries.at[:, :, cols], q_in.at[s, :, rows, :]),
            (keys.at[1, :, cols], kv1.at[s, 0, 0, rows, :]),
            (values.at[1, :, cols], v1_in.at[s, 0, rows, :]),
        )

    def far_pieces(s, target_place, source_place):
        cols = columns_of(4 * s + target_place)
        rows = rows_of(source_place)
        return (
            (keys.at[1, :, cols], kv1.at[s, 1, 0, rows, :]),
            (values.at[1, :, cols], v1_in.at[s, 1, rows, :]),
        )

    mine = []
    for group in ((0, 1), (2,), (3, 4)):
        for step in (1, 3, 2):
            for s in range(SLOTS):
                axis = SPREAD[s]
                place = shifted(axis, step)
                both = pieces(s, place, at[axis])
                for n in group:
                    sent.append(remote(
                        *both[n], ex_send.at[s, step, n], ex_recv.at[s, step, n], device(**{axis: place})
                    ))
        for s in range(SLOTS):
            both = pieces(s, at[SPREAD[s]], at[SPREAD[s]])
            for n in group:
                copy = pltpu.make_async_copy(*both[n], local.at[s * 5 + n])
                copy.start()
                mine.append((n, copy))
    for step in range(RING):
        for s in (1, 2):
            axis = SPREAD[s]
            place = shifted(axis, step)
            both = far_pieces(s, place, at[axis])
            for n in range(2):
                sent.append(remote(
                    *both[n], ex_send.at[s, step, 5 + n], ex_recv.at[s, step, 5 + n],
                    device(y=far_y, **{axis: place}),
                ))

    fetched = []
    for n, (src, dst) in enumerate(((weight, w_buf), (hidden, h_buf), (gates, g_buf))):
        copy = pltpu.make_async_copy(src, dst, local.at[15 + n])
        copy.start()
        fetched.append(copy)

    top[...] = jnp.full(top.shape, LOWEST, jnp.float32)
    total[...] = jnp.zeros(total.shape, jnp.float32)
    acc[...] = jnp.zeros(acc.shape, jnp.float32)

    def exchanged(s, n):
        for step in (1, 3, 2):
            source = shifted(SPREAD[s], RING - step)
            src, dst = pieces(s, at[SPREAD[s]], source)[n]
            remote(src, dst, ex_send.at[s, step, n], ex_recv.at[s, step, n], sibling, start=False).wait_recv()

    def far_exchanged(s, n):
        for step in range(RING):
            source = shifted(SPREAD[s], RING - step)
            src, dst = far_pieces(s, at[SPREAD[s]], source)[n]
            remote(
                src, dst, ex_send.at[s, step, 5 + n], ex_recv.at[s, step, 5 + n], sibling, start=False
            ).wait_recv()

    def blocks_transposed(block):
        return jnp.concatenate([block[n * HD:(n + 1) * HD].T for n in range(CHUNK // HD)], axis=0)

    def chunk(s, first, second, half=None):
        where = kv.at[s, chip_routed(s, first, second), core]
        return where if half is None else where.at[half]

    slot_sends = [0] * SLOTS

    def pass_on(s, first, second, which, step, half=None):
        there = (first - step, second) if which == 0 else (first, second - step)
        there = (there[0] % RING, there[1] % RING)
        ref = chunk(s, first, second, half)
        n = slot_sends[s]
        slot_sends[s] += 1
        remote(
            ref, ref, ag_send.at[s, n],
            ag_recv.at[s, there[0], there[1], 0 if half is None else half],
            routed(s, which, step),
        )
        gathered.append((s, n, first, second, half))

    def to_sibling(s, first, second):
        ref = chunk(s, first, second)
        n = slot_sends[s]
        slot_sends[s] += 1
        place = pick(first * RING + second, second * RING + first)
        remote(ref, ref, ag_send.at[s, n], sib_recv.at[s, place], sibling)
        gathered.append((s, n, first, second, None))

    def arrive(s, first, second):
        across = first if second == 0 else second
        for half in (0, 1) if across == 2 else (None,):
            ref = chunk(s, first, second, half)
            remote(
                ref, ref, ag_send.at[s, 0],
                ag_recv.at[s, first, second, 0 if half is None else half], sibling, start=False,
            ).wait_recv()
        if second == 0:
            if first == 3:
                pass_on(s, first, second, 0, 1, 0)
            elif first == 1:
                pass_on(s, first, second, 0, 3, 1)
            pass_on(s, first, second, 1, 1)
            pass_on(s, first, second, 1, 3)
        elif second == 3:
            pass_on(s, first, second, 1, 1, 0)
        elif second == 1:
            pass_on(s, first, second, 1, 3, 1)
        to_sibling(s, first, second)

    def other_half(s, da, db):
        ref = kv.at[s, chip_at(s, da, db), 1 - core]
        remote(
            ref, ref, ag_send.at[s, 0], sib_recv.at[s, da * RING + db], sibling, start=False
        ).wait_recv()

    def masked(s, first_column, width):
        row = block_of(lax.broadcasted_iota(jnp.int32, (CHUNK, width), 0))
        column = lax.broadcasted_iota(jnp.int32, (CHUNK, width), 1) + (first_column - CHUNK)
        block = block_of(column)
        if s == 0:
            same = lax.rem(row, 2) == lax.rem(block, 2)
        else:
            same = row == block
        return same & (column >= 0)

    def soften(s, cols, scores):
        old = top[s, :, cols]
        new = jnp.maximum(old, jnp.max(scores, axis=0, keepdims=True))
        top[s, :, cols] = new
        fade = jnp.exp2((old - new) * LOG2_SCALE)
        lifted = jnp.exp2((scores - new) * LOG2_SCALE)
        total[s, :, cols] = total[s, :, cols] * fade + jnp.sum(lifted, axis=0, keepdims=True)
        return lifted.astype(jnp.bfloat16), fade

    def weigh(s, cols, value_block, lifted, fade):
        acc[s, :, cols] = acc[s, :, cols] * fade + jnp.dot(
            value_block, lifted, preferred_element_type=jnp.float32
        )

    def visit(chips, masked_slots):
        work = [(s, t) for s in range(SLOTS) for t in range(QUERIES // TILE)]
        scores, lifted = {}, {}
        for j in range(len(work) + 2):
            if j >= 2:
                s, t = work[j - 2]
                cols = slice(t * TILE, (t + 1) * TILE)
                value_block = jnp.concatenate(
                    [
                        kv[s, chips[s], half, 1, n * HD:(n + 1) * HD, :]
                        for half in (core, 1 - core)
                        for n in range(CHUNK // HD)
                    ],
                    axis=1,
                )
                weigh(s, cols, value_block, *lifted.pop(j - 2))
            if j < len(work):
                s, t = work[j]
                cols = slice(t * TILE, (t + 1) * TILE)
                key_block = jnp.concatenate(
                    [kv[s, chips[s], half, 0] for half in (core, 1 - core)], axis=0
                )
                scores[j] = jnp.dot(key_block, qt[s, :, cols], preferred_element_type=jnp.float32)
            if 1 <= j <= len(work):
                s, t = work[j - 1]
                cols = slice(t * TILE, (t + 1) * TILE)
                block = scores.pop(j - 1)
                if s in masked_slots and (t + 1) * TILE > CHUNK:
                    hide = masked(s, t * TILE, TILE)
                    block = jnp.concatenate(
                        [jnp.where(hide, LOWEST, block[:CHUNK]), block[CHUNK:]], axis=0
                    )
                lifted[j - 1] = soften(s, cols, block)

    def visit_replaced(s, w):
        cols = slice(CHUNK, QUERIES)
        block = jnp.dot(kv1[s, w, 0], qt[s, :, cols], preferred_element_type=jnp.float32)
        block = jnp.where(masked(s, CHUNK, CHUNK), block, LOWEST)
        value_block = jnp.concatenate(
            [kv1[s, w, 1, n * HD:(n + 1) * HD, :] for n in range(CHUNK // HD)], axis=1
        )
        weigh(s, cols, value_block, *soften(s, cols, block))

    for n, copy in mine:
        if n < 2:
            copy.wait()
    for s in range(SLOTS):
        exchanged(s, 0)
        exchanged(s, 1)
        kv[s, own_chip(s), core, 1] = blocks_transposed(v_in[s])
        to_sibling(s, 0, 0)
        for step in (1, 3):
            pass_on(s, 0, 0, 0, step)
            pass_on(s, 0, 0, 1, step)

    for n, copy in mine:
        if n >= 2:
            copy.wait()
    for s in range(SLOTS):
        exchanged(s, 2)
        for step in range(2):
            for n in range(CHUNK // HD):
                start = step * CHUNK + n * HD
                qt[s, :, start:start + HD] = q_in[s, step, n * HD:(n + 1) * HD, :].T
    for s in range(SLOTS):
        other_half(s, 0, 0)
    visit([own_chip(s) for s in range(SLOTS)], (0, 1, 2))
    for s in range(SLOTS):
        for w in (0,) if s == 0 else (0, 1):
            for n in range(2):
                if w == 0:
                    exchanged(s, 3 + n)
                else:
                    far_exchanged(s, n)
            kv1[s, w, 1] = blocks_transposed(v1_in[s, w])
            visit_replaced(s, w)

    def turn(r, carry):
        for at_visit, arrivals in ARRIVALS.items():
            @pl.when(r == at_visit)
            def _():
                for place in arrivals:
                    for s in range(SLOTS):
                        arrive(s, *place)

        da = sum((r == n).astype(jnp.int32) * place[0] for n, place in enumerate(VISITS))
        db = sum((r == n).astype(jnp.int32) * place[1] for n, place in enumerate(VISITS))
        for s in range(SLOTS):
            other_half(s, da, db)
        visit([chip_at(s, da, db) for s in range(SLOTS)], ())
        return carry

    lax.fori_loop(0, len(VISITS), turn, 0)

    for s in range(SLOTS):
        other_half(s, *PARTNER)
    visit([chip_at(s, *PARTNER) for s in range(SLOTS)], (1, 2))

    returns = []
    for s in range(SLOTS):
        axis = SPREAD[s]
        result = (acc[s] / total[s]).astype(jnp.bfloat16)
        for step in range(2):
            o_out[s, step] = jnp.concatenate(
                [
                    result[:, step * CHUNK + n * HD:step * CHUNK + (n + 1) * HD].T
                    for n in range(CHUNK // HD)
                ],
                axis=0,
            )
        cols = columns_of(4 * s + at[axis])
        for step in (2, 1, 3):
            place = shifted(axis, step)
            sent.append(remote(
                o_out.at[s, :, rows_of(place), :], att.at[:, :, cols],
                ret_send.at[s, step], ret_recv.at[s, step], device(**{axis: place}),
            ))
        copy = pltpu.make_async_copy(o_out.at[s, :, rows_of(at[axis]), :], att.at[:, :, cols], local.at[18 + s])
        copy.start()
        returns.append(copy)
    for copy in fetched + returns:
        copy.wait()
    for s in range(SLOTS):
        axis = SPREAD[s]
        for step in (1, 3, 2):
            source = shifted(axis, RING - step)
            remote(
                o_out.at[s, :, rows_of(at[axis]), :], att.at[:, :, columns_of(4 * s + source)],
                ret_send.at[s, step], ret_recv.at[s, step], sibling, start=False,
            ).wait_recv()

    merged = att[...].reshape(2 * TOK, att.shape[2])
    width = out.shape[2]
    for n in range(0, width, 512):
        cols = slice(n, n + 512)
        projected = jnp.dot(merged, w_buf[:, cols], preferred_element_type=jnp.float32)
        for step in range(2):
            gate = g_buf[pl.ds(steps[step], 1), cols]
            block = projected[step * TOK:(step + 1) * TOK]
            out[step, :, cols] = (h_buf[step, :, cols].astype(jnp.float32) + gate * block).astype(out.dtype)

    for copy in sent:
        copy.wait_send()
    for s, n, first, second, half in gathered:
        ref = chunk(s, first, second, half)
        remote(ref, ref, ag_send.at[s, n], ag_recv.at[s, 0, 0, 0], sibling, start=False).wait_send()


def shards(hidden, queries, keys, values, out_weight, gate_table, steps_t):
    any_spec = pl.BlockSpec(memory_space=pl.ANY)
    dma = pltpu.SemaphoreType.DMA
    bf16, f32 = jnp.bfloat16, jnp.float32
    return pl.pallas_call(
        kernel,
        out_shape=jax.ShapeDtypeStruct(hidden.shape, hidden.dtype),
        in_specs=[any_spec] * 6 + [pl.BlockSpec(memory_space=pltpu.SMEM)],
        out_specs=pl.BlockSpec(memory_space=pltpu.VMEM),
        scratch_shapes=[
            pltpu.VMEM((SLOTS, RING * RING, 2, 2, CHUNK, HD), bf16),
            pltpu.VMEM((SLOTS, 2, 2, CHUNK, HD), bf16),
            pltpu.VMEM((SLOTS, CHUNK, HD), bf16),
            pltpu.VMEM((SLOTS, 2, CHUNK, HD), bf16),
            pltpu.VMEM((SLOTS, 2, CHUNK, HD), bf16),
            pltpu.VMEM((SLOTS, HD, QUERIES), bf16),
            pltpu.VMEM((SLOTS, HD, QUERIES), f32),
            pltpu.VMEM((SLOTS, 1, QUERIES), f32),
            pltpu.VMEM((SLOTS, 1, QUERIES), f32),
            pltpu.VMEM((SLOTS, 2, CHUNK, HD), bf16),
            pltpu.VMEM(queries.shape, bf16),
            pltpu.VMEM(out_weight.shape, bf16),
            pltpu.VMEM(gate_table.shape, f32),
            pltpu.VMEM(hidden.shape, bf16),
            dma((SLOTS, RING, 7)),
            dma((SLOTS, RING, 7)),
            dma((SLOTS, 36)),
            dma((SLOTS, RING, RING, 2)),
            dma((SLOTS, RING * RING)),
            dma((SLOTS, RING)),
            dma((SLOTS, RING)),
            dma((21,)),
        ],
        compiler_params=pltpu.CompilerParams(
            collective_id=0, has_side_effects=True, vmem_limit_bytes=58 * 2**20
        ),
        name="attend",
    )(hidden, queries, keys, values, out_weight, gate_table, steps_t)


def solution(mesh):
    rows = P(None, ("patch", "head"), None)
    return jax.shard_map(
        shards,
        mesh=mesh,
        in_specs=(rows, rows, rows, rows, P(), P(), P()),
        out_specs=rows,
        check_vma=False,
    )
```

```python
import functools
import math

import jax
import jax.numpy as jnp
from jax import lax
from jax.experimental import pallas as pl
from jax.experimental.pallas import tpu as pltpu
from jax.sharding import PartitionSpec as P

HD = 128
TOK = 96
CHUNK = 4 * TOK
QUERIES = 2 * CHUNK
RING = 4
SLOTS = 3
TILE = 256
LOG2_SCALE = math.log2(math.e) / math.sqrt(HD)
LOWEST = -1e30
SUMS = 16

SPREAD = ("y", "x", "z")
PLANE = (("x", "z"), ("y", "z"), ("y", "x"))

VISITS = (
    ((1, 0), (3, 0)), ((0, 1), (0, 3)), ((1, 1), (1, 3)), ((3, 1), (3, 3)),
    ((2, 1), (2, 3)), (None, (1, 2)), ((3, 2), (2, 2)),
)
FREE = (0, 2)
PARTNER = (2, 0)

ARRIVALS = {
    0: ((1, 0), (3, 0)),
    2: ((0, 1), (0, 3)),
    3: ((2, 0),),
    4: ((1, 1), (1, 3)),
    6: ((3, 1), (3, 3)),
    8: ((2, 1), (2, 3), (0, 2)),
    10: ((1, 2),),
    12: ((3, 2), (2, 2)),
}
PASSES = {
    0: (
        ((0, 0), 1, 1, None), ((0, 0), 1, 3, None),
        ((3, 0), 0, 1, 0), ((1, 0), 0, 3, 1),
    ),
    1: (((1, 0), 1, 1, None), ((1, 0), 1, 3, None)),
    3: (((3, 0), 1, 1, None), ((3, 0), 1, 3, None)),
    4: (((0, 3), 1, 1, 0), ((0, 1), 1, 3, 1)),
    5: (((2, 0), 1, 1, None), ((2, 0), 1, 3, None)),
    6: (((1, 3), 1, 1, 0), ((1, 1), 1, 3, 1)),
    7: (((3, 3), 1, 1, 0), ((3, 1), 1, 3, 1)),
    8: (((2, 3), 1, 1, 0), ((2, 1), 1, 3, 1)),
}
HAND_ON = 6


def block_of(index):
    return sum((index >= edge * TOK).astype(jnp.int32) for edge in range(1, RING))


def kernel(
    hidden, queries, keys, values, weight, gates, steps, out,
    kv, kv1, v_in, v1_in, q_in, qt, acc, top, part, level, o_out, att, w_buf, g_buf, h_buf,
    ex_send, ex_recv, ag_send, ag_recv, sib_send, sib_recv, far_send, far_recv, ret_send, ret_recv, local,
):
    patch, head = lax.axis_index("patch"), lax.axis_index("head")
    core = lax.rem(patch, 2)
    at = {
        "x": patch // 16,
        "z": lax.rem(patch // 4, RING),
        "y": head * 2 + lax.rem(patch // 2, 2),
    }

    def device(**moved):
        pos = dict(at, core=core)
        pos.update(moved)
        y = pos["y"]
        return (((pos["x"] * RING + pos["z"]) * 2 + lax.rem(y, 2)) * 2 + pos["core"], y // 2)

    def shifted(axis, step):
        return lax.rem(at[axis] + step, RING)

    def pick(first, second):
        return first + core * (second - first)

    def routed(s, which, step):
        a, b = PLANE[s] if which == 0 else PLANE[s][::-1]
        da, db = device(**{a: shifted(a, step)}), device(**{b: shifted(b, step)})
        return (pick(da[0], db[0]), pick(da[1], db[1]))

    def chip_at(s, da, db):
        a, b = PLANE[s]
        return shifted(a, da) * RING + shifted(b, db)

    def chip_routed(s, first, second):
        return pick(chip_at(s, first, second), chip_at(s, second, first))

    sibling = device(core=1 - core)
    far_y = shifted("y", 2)

    peers = [device(**{axis: shifted(axis, step)}) for axis in "xyz" for step in (1, 2, 3)]
    peers.append(sibling)
    barrier = pltpu.get_barrier_semaphore()
    for peer in peers:
        pl.semaphore_signal(barrier, inc=1, device_id=peer, device_id_type=pl.DeviceIdType.MESH)

    sent, gathered = [], []

    def remote(src, dst, send_sem, recv_sem, target, start=True):
        copy = pltpu.make_async_remote_copy(
            src_ref=src, dst_ref=dst, send_sem=send_sem, recv_sem=recv_sem,
            device_id=target, device_id_type=pl.DeviceIdType.MESH,
        )
        if start:
            copy.start()
        return copy

    def rows_of(place):
        return pl.ds(pl.multiple_of(place * TOK, TOK), TOK)

    def columns_of(place):
        return pl.ds(pl.multiple_of(place * HD, HD), HD)

    def own_chip(s):
        return chip_at(s, 0, 0)

    def pieces(s, target_place, source_place):
        cols = columns_of(4 * s + target_place)
        rows = rows_of(source_place)
        return (
            (keys.at[0, :, cols], kv.at[s, own_chip(s), 0, rows, :]),
            (values.at[0, :, cols], v_in.at[s, rows, :]),
            (queries.at[:, :, cols], q_in.at[0, s, :, rows, :]),
            (keys.at[1, :, cols], kv1.at[s, 0, 0, rows, :]),
            (values.at[1, :, cols], v1_in.at[s, rows, :]),
        )

    def exchange(group):
        for step in (1, 3, 2):
            for s in range(SLOTS):
                axis = SPREAD[s]
                place = shifted(axis, step)
                both = pieces(s, place, at[axis])
                for n in group:
                    sent.append(remote(
                        *both[n], ex_send.at[s, step, n], ex_recv.at[s, step, n], device(**{axis: place})
                    ))

    mine = []
    for n in range(5):
        for s in range(SLOTS):
            copy = pltpu.make_async_copy(*pieces(s, at[SPREAD[s]], at[SPREAD[s]])[n], local.at[s * 5 + n])
            copy.start()
            mine.append((n, copy))
    fetched = []
    for n, (src, dst) in enumerate(((weight, w_buf), (hidden, h_buf), (gates, g_buf))):
        copy = pltpu.make_async_copy(src, dst, local.at[15 + n])
        copy.start()
        fetched.append(copy)

    top[...] = jnp.full(top.shape, LOWEST, jnp.float32)
    acc[...] = jnp.zeros(acc.shape, jnp.float32)

    pl.semaphore_wait(barrier, len(peers))
    exchange((0, 1))
    exchange((2,))

    def exchanged(s, n):
        for step in (1, 3, 2):
            source = shifted(SPREAD[s], RING - step)
            src, dst = pieces(s, at[SPREAD[s]], source)[n]
            remote(src, dst, ex_send.at[s, step, n], ex_recv.at[s, step, n], sibling, start=False).wait_recv()

    def blocks_transposed(block):
        return jnp.concatenate([block[n * HD:(n + 1) * HD].T for n in range(CHUNK // HD)], axis=0)

    def chunk(s, first, second, half=None):
        where = kv.at[s, chip_routed(s, first, second)]
        return where if half is None else where.at[half]

    slot_sends = [0] * SLOTS

    def pass_on(s, first, second, which, step, half=None):
        there = (first - step, second) if which == 0 else (first, second - step)
        there = (there[0] % RING, there[1] % RING)
        ref = chunk(s, first, second, half)
        n = slot_sends[s]
        slot_sends[s] += 1
        remote(
            ref, ref, ag_send.at[s, n],
            ag_recv.at[s, there[0], there[1], 0 if half is None else half],
            routed(s, which, step),
        )
        gathered.append((s, n, first, second, half))

    def arrive(s, first, second):
        across = first if second == 0 else second
        for half in (0, 1) if across == 2 else (None,):
            ref = chunk(s, first, second, half)
            remote(
                ref, ref, ag_send.at[s, 0],
                ag_recv.at[s, first, second, 0 if half is None else half], sibling, start=False,
            ).wait_recv()

    def to_sibling(n, src, dst):
        return remote(src, dst, sib_send.at[n], sib_recv.at[n], sibling, start=False)

    def sibling_queries(s):
        return to_sibling(s, q_in.at[0, s], q_in.at[1, s])

    def partial(s):
        return (
            to_sibling(3 + 2 * s, part.at[0, s], part.at[1, s]),
            to_sibling(4 + 2 * s, level.at[0, s], level.at[1, s]),
        )

    def masked(s, first_column, width):
        row = block_of(lax.broadcasted_iota(jnp.int32, (CHUNK, width), 0))
        column = lax.broadcasted_iota(jnp.int32, (CHUNK, width), 1) + (first_column - CHUNK)
        block = block_of(column)
        if s == 0:
            same = lax.rem(row, 2) == lax.rem(block, 2)
        else:
            same = row == block
        return same & (column >= 0)

    def soften(q, s, cols, scores):
        old = top[q, s, :, cols]
        new = jnp.maximum(old, jnp.max(scores, axis=0, keepdims=True))
        top[q, s, :, cols] = new
        return jnp.exp2(scores - new).astype(jnp.bfloat16), jnp.exp2(old - new)

    def score(q, s, cols, key_block):
        return jnp.dot(
            jnp.concatenate([key_block, key_block], axis=1), qt[q, s, :, cols],
            preferred_element_type=jnp.float32,
        )

    def weigh(q, s, cols, value_blocks, lifted, fade):
        value_block = jnp.concatenate(value_blocks, axis=1)
        ones = jnp.ones((SUMS, value_block.shape[1]), value_block.dtype)
        acc[q, s, :, cols] = acc[q, s, :, cols] * fade + jnp.dot(
            jnp.concatenate([value_block, ones], axis=0), lifted, preferred_element_type=jnp.float32
        )

    def visit(q, chips, masked_slots):
        work = [(s, slice(t, t + TILE)) for s in range(SLOTS) for t in range(0, QUERIES, TILE)]
        scores, lifted = {}, {}
        for j in range(len(work) + 2):
            if j >= 2:
                s, cols = work[j - 2]
                value_blocks = [
                    kv[s, chip, 1, n * HD:(n + 1) * HD, :] for chip in chips[s] for n in range(CHUNK // HD)
                ]
                weigh(q, s, cols, value_blocks, *lifted.pop(j - 2))
            if j < len(work):
                s, cols = work[j]
                key_block = jnp.concatenate([kv[s, chip, 0] for chip in chips[s]], axis=0)
                scores[j] = score(q, s, cols, key_block)
            if 1 <= j <= len(work):
                s, cols = work[j - 1]
                block = scores.pop(j - 1)
                if s in masked_slots and cols.stop > CHUNK:
                    block = jnp.where(masked(s, cols.start, TILE), LOWEST, block)
                lifted[j - 1] = soften(q, s, cols, block)

    def visit_replaced(s, w):
        cols = slice(CHUNK, QUERIES)
        block = score(0, s, cols, kv1[s, w, 0])
        block = jnp.where(masked(s, CHUNK, CHUNK), block, LOWEST)
        value_blocks = [kv1[s, w, 1, n * HD:(n + 1) * HD, :] for n in range(CHUNK // HD)]
        weigh(0, s, cols, value_blocks, *soften(0, s, cols, block))

    def turn_queries(q):
        for s in range(SLOTS):
            for step in range(2):
                for n in range(CHUNK // HD):
                    start = step * CHUNK + n * HD
                    scaled = q_in[q, s, step, n * HD:(n + 1) * HD, :].astype(jnp.float32).T * LOG2_SCALE
                    high = scaled.astype(jnp.bfloat16)
                    qt[q, s, :HD, start:start + HD] = high
                    qt[q, s, HD:, start:start + HD] = (scaled - high.astype(jnp.float32)).astype(jnp.bfloat16)

    for n, copy in mine:
        if n < 2:
            copy.wait()
    for s in range(SLOTS):
        exchanged(s, 0)
        exchanged(s, 1)
        kv[s, own_chip(s), 1] = blocks_transposed(v_in[s])
        for step in (1, 3):
            pass_on(s, 0, 0, 0, step)

    for n, copy in mine:
        if n >= 2:
            copy.wait()
    for s in range(SLOTS):
        exchanged(s, 2)
        sibling_queries(s).start()
    exchange((3, 4))
    turn_queries(0)
    own = [(own_chip(s),) for s in range(SLOTS)]
    visit(0, own, (0, 1, 2))
    for s in range(SLOTS):
        sibling_queries(s).wait_recv()
    turn_queries(1)
    visit(1, own, ())

    def replacement(s):
        ref = kv1.at[s, 0]
        return remote(
            ref, kv1.at[s, 1], far_send.at[s], far_recv.at[s], device(y=far_y), start=False
        )

    def hand_on():
        for s in range(SLOTS):
            exchanged(s, 3)
            exchanged(s, 4)
            kv1[s, 0, 1] = blocks_transposed(v1_in[s])
            if s > 0:
                replacement(s).start()

    def turn(r, carry):
        for k in range(2 * len(VISITS)):
            if k in ARRIVALS or k in PASSES:
                @pl.when(r == k)
                def _():
                    for s in range(SLOTS):
                        for place in ARRIVALS.get(k, ()):
                            arrive(s, *place)
                    for place, which, step, half in PASSES.get(k, ()):
                        for s in range(SLOTS):
                            pass_on(s, *place, which, step, half)

        pl.when(r == HAND_ON)(hand_on)
        pair = r // 2
        chips = []
        for s in range(SLOTS):
            places = [
                [
                    chip_at(s, *FREE) if place is None else chip_routed(s, *place)
                    for place in (visited[side] for visited in VISITS)
                ]
                for side in range(2)
            ]
            chips.append([
                sum((pair == n).astype(jnp.int32) * place for n, place in enumerate(places[side]))
                for side in range(2)
            ])
        visit(lax.rem(r, 2), chips, ())
        return carry

    lax.fori_loop(0, 2 * len(VISITS), turn, 0)

    partner = [(chip_at(s, *PARTNER),) for s in range(SLOTS)]
    visit(1, partner, ())
    for s in range(SLOTS):
        weight_sum = acc[1, s, HD:HD + 1]
        part[0, s] = (acc[1, s, :HD] / weight_sum).astype(jnp.bfloat16)
        level[0, s] = jnp.broadcast_to(top[1, s] + jnp.log2(weight_sum), level.shape[2:])
        for copy in partial(s):
            copy.start()
    visit(0, partner, (1, 2))
    for s in range(SLOTS):
        visit_replaced(s, 0)
        if s > 0:
            replacement(s).wait_recv()
            visit_replaced(s, 1)

    returns = []
    for s in range(SLOTS):
        axis = SPREAD[s]
        for copy in partial(s):
            copy.wait_recv()
        weight_sum = acc[0, s, HD:HD + 1]
        gap = level[1, s, 0:1] - (top[0, s] + jnp.log2(weight_sum))
        result = (
            acc[0, s, :HD] / (weight_sum * (1.0 + jnp.exp2(gap)))
            + part[1, s].astype(jnp.float32) / (1.0 + jnp.exp2(-gap))
        ).astype(jnp.bfloat16)
        for step in range(2):
            o_out[s, step] = jnp.concatenate(
                [
                    result[:, step * CHUNK + n * HD:step * CHUNK + (n + 1) * HD].T
                    for n in range(CHUNK // HD)
                ],
                axis=0,
            )
        cols = columns_of(4 * s + at[axis])
        for step in (2, 1, 3):
            place = shifted(axis, step)
            sent.append(remote(
                o_out.at[s, :, rows_of(place), :], att.at[:, :, cols],
                ret_send.at[s, step], ret_recv.at[s, step], device(**{axis: place}),
            ))
        copy = pltpu.make_async_copy(o_out.at[s, :, rows_of(at[axis]), :], att.at[:, :, cols], local.at[18 + s])
        copy.start()
        returns.append(copy)
    for copy in fetched + returns:
        copy.wait()
    for s in range(SLOTS):
        axis = SPREAD[s]
        for step in (1, 3, 2):
            source = shifted(axis, RING - step)
            remote(
                o_out.at[s, :, rows_of(at[axis]), :], att.at[:, :, columns_of(4 * s + source)],
                ret_send.at[s, step], ret_recv.at[s, step], sibling, start=False,
            ).wait_recv()

    merged = att[...].reshape(2 * TOK, att.shape[2])
    width = out.shape[2]
    for n in range(0, width, 512):
        cols = slice(n, n + 512)
        projected = jnp.dot(merged, w_buf[:, cols], preferred_element_type=jnp.float32)
        for step in range(2):
            gate = g_buf[pl.ds(steps[step], 1), cols]
            block = projected[step * TOK:(step + 1) * TOK]
            out[step, :, cols] = (h_buf[step, :, cols].astype(jnp.float32) + gate * block).astype(out.dtype)

    for copy in sent:
        copy.wait_send()
    for s in (1, 2):
        replacement(s).wait_send()
    for s in range(SLOTS):
        for copy in (sibling_queries(s),) + partial(s):
            copy.wait_send()
    for s, n, first, second, half in gathered:
        ref = chunk(s, first, second, half)
        remote(ref, ref, ag_send.at[s, n], ag_recv.at[s, 0, 0, 0], sibling, start=False).wait_send()


def shards(hidden, queries, keys, values, out_weight, gate_table, steps_t):
    any_spec = pl.BlockSpec(memory_space=pl.ANY)
    dma = pltpu.SemaphoreType.DMA
    bf16, f32 = jnp.bfloat16, jnp.float32
    return pl.pallas_call(
        kernel,
        out_shape=jax.ShapeDtypeStruct(hidden.shape, hidden.dtype),
        in_specs=[any_spec] * 6 + [pl.BlockSpec(memory_space=pltpu.SMEM)],
        out_specs=pl.BlockSpec(memory_space=pltpu.VMEM),
        scratch_shapes=[
            pltpu.VMEM((SLOTS, RING * RING, 2, CHUNK, HD), bf16),
            pltpu.VMEM((SLOTS, 2, 2, CHUNK, HD), bf16),
            pltpu.VMEM((SLOTS, CHUNK, HD), bf16),
            pltpu.VMEM((SLOTS, CHUNK, HD), bf16),
            pltpu.VMEM((2, SLOTS, 2, CHUNK, HD), bf16),
            pltpu.VMEM((2, SLOTS, 2 * HD, QUERIES), bf16),
            pltpu.VMEM((2, SLOTS, HD + SUMS, QUERIES), f32),
            pltpu.VMEM((2, SLOTS, 1, QUERIES), f32),
            pltpu.VMEM((2, SLOTS, HD, QUERIES), bf16),
            pltpu.VMEM((2, SLOTS, 8, QUERIES), f32),
            pltpu.VMEM((SLOTS, 2, CHUNK, HD), bf16),
            pltpu.VMEM(queries.shape, bf16),
            pltpu.VMEM(out_weight.shape, bf16),
            pltpu.VMEM(gate_table.shape, f32),
            pltpu.VMEM(hidden.shape, bf16),
            dma((SLOTS, RING, 5)),
            dma((SLOTS, RING, 5)),
            dma((SLOTS, 20)),
            dma((SLOTS, RING, RING, 2)),
            dma((9,)),
            dma((9,)),
            dma((SLOTS,)),
            dma((SLOTS,)),
            dma((SLOTS, RING)),
            dma((SLOTS, RING)),
            dma((21,)),
        ],
        compiler_params=pltpu.CompilerParams(
            collective_id=0, has_side_effects=True, vmem_limit_bytes=58 * 2**20
        ),
        name="attend",
    )(hidden, queries, keys, values, out_weight, gate_table, steps_t)


def solution(mesh):
    rows = P(None, ("patch", "head"), None)
    return jax.shard_map(
        shards,
        mesh=mesh,
        in_specs=(rows, rows, rows, rows, P(), P(), P()),
        out_specs=rows,
        check_vma=False,
    )
```

```python
import functools
import math

import jax
import jax.numpy as jnp
from jax import lax
from jax.experimental import pallas as pl
from jax.experimental.pallas import tpu as pltpu
from jax.sharding import PartitionSpec as P

HD = 128
TOK = 96
CHUNK = 4 * TOK
QUERIES = 2 * CHUNK
RING = 4
SLOTS = 3
TILE = 256
LOG2_SCALE = math.log2(math.e) / math.sqrt(HD)
LOWEST = -1e30
SUMS = 16

SPREAD = ("y", "x", "z")
PLANE = (("x", "z"), ("y", "z"), ("y", "x"))

VISITS = (
    ((1, 0), (3, 0)), ((0, 1), (0, 3)), ((1, 1), (1, 3)), ((3, 1), (3, 3)),
    ((2, 1), (2, 3)), (None, (1, 2)), ((3, 2), (2, 2)),
)
FREE = (0, 2)
PARTNER = (2, 0)

ARRIVALS = {
    0: ((1, 0), (3, 0)),
    2: ((0, 1), (0, 3)),
    4: ((1, 1), (1, 3)),
    5: ((2, 0),),
    6: ((3, 1), (3, 3)),
    8: ((2, 1), (2, 3)),
    10: ((0, 2), (1, 2)),
    12: ((3, 2), (2, 2)),
}
PASSES = {
    0: (
        ((0, 0), 1, 1, None), ((0, 0), 1, 3, None),
        ((3, 0), 0, 1, 0), ((1, 0), 0, 3, 1),
    ),
    1: (((1, 0), 1, 1, None), ((1, 0), 1, 3, None)),
    3: (((3, 0), 1, 1, None), ((3, 0), 1, 3, None)),
    4: (((0, 3), 1, 1, 0), ((0, 1), 1, 3, 1)),
    5: (((2, 0), 1, 1, None), ((2, 0), 1, 3, None)),
    6: (((1, 3), 1, 1, 0), ((1, 1), 1, 3, 1)),
    7: (((3, 3), 1, 1, 0), ((3, 1), 1, 3, 1)),
    8: (((2, 3), 1, 1, 0), ((2, 1), 1, 3, 1)),
}
HAND_ON = 10
WITH_PARTNER = 10


def block_of(index):
    return sum((index >= edge * TOK).astype(jnp.int32) for edge in range(1, RING))


def kernel(
    hidden, queries, keys, values, weight, gates, steps, out,
    kv, kv1, between, v_in, v1_in, q_in, qt, acc, top, part, level, o_out, att, w_buf, g_buf, h_buf,
    ex_send, ex_recv, ag_send, ag_recv, sib_send, sib_recv, far_send, far_recv, ret_send, ret_recv, local,
):
    patch, head = lax.axis_index("patch"), lax.axis_index("head")
    core = lax.rem(patch, 2)
    at = {
        "x": patch // 16,
        "z": lax.rem(patch // 4, RING),
        "y": head * 2 + lax.rem(patch // 2, 2),
    }

    def device(**moved):
        pos = dict(at, core=core)
        pos.update(moved)
        y = pos["y"]
        return (((pos["x"] * RING + pos["z"]) * 2 + lax.rem(y, 2)) * 2 + pos["core"], y // 2)

    def shifted(axis, step):
        return lax.rem(at[axis] + step, RING)

    def pick(first, second):
        return first + core * (second - first)

    def routed(s, which, step):
        a, b = PLANE[s] if which == 0 else PLANE[s][::-1]
        da, db = device(**{a: shifted(a, step)}), device(**{b: shifted(b, step)})
        return (pick(da[0], db[0]), pick(da[1], db[1]))

    def chip_at(s, da, db):
        a, b = PLANE[s]
        return shifted(a, da) * RING + shifted(b, db)

    def chip_routed(s, first, second):
        return pick(chip_at(s, first, second), chip_at(s, second, first))

    sibling = device(core=1 - core)

    peers = [device(**{axis: shifted(axis, step)}) for axis in "xyz" for step in (1, 2, 3)]
    peers.append(sibling)
    barrier = pltpu.get_barrier_semaphore()
    for peer in peers:
        pl.semaphore_signal(barrier, inc=1, device_id=peer, device_id_type=pl.DeviceIdType.MESH)

    sent, gathered = [], []

    def remote(src, dst, send_sem, recv_sem, target, start=True):
        copy = pltpu.make_async_remote_copy(
            src_ref=src, dst_ref=dst, send_sem=send_sem, recv_sem=recv_sem,
            device_id=target, device_id_type=pl.DeviceIdType.MESH,
        )
        if start:
            copy.start()
        return copy

    def rows_of(place):
        return pl.ds(pl.multiple_of(place * TOK, TOK), TOK)

    def columns_of(place):
        return pl.ds(pl.multiple_of(place * HD, HD), HD)

    def own_chip(s):
        return chip_at(s, 0, 0)

    def pieces(s, target_place, source_place):
        cols = columns_of(4 * s + target_place)
        rows = rows_of(source_place)
        return (
            (keys.at[0, :, cols], kv.at[s, own_chip(s), 0, rows, :]),
            (values.at[0, :, cols], v_in.at[s, rows, :]),
            (queries.at[:, :, cols], q_in.at[0, s, :, rows, :]),
            (keys.at[1, :, cols], kv1.at[s, 0, 0, rows, :]),
            (values.at[1, :, cols], v1_in.at[s, rows, :]),
        )

    def exchange(group):
        for step in (1, 3, 2):
            for s in range(SLOTS):
                axis = SPREAD[s]
                place = shifted(axis, step)
                both = pieces(s, place, at[axis])
                for n in group:
                    sent.append(remote(
                        *both[n], ex_send.at[s, step, n], ex_recv.at[s, step, n], device(**{axis: place})
                    ))

    mine = []
    for n in range(5):
        for s in range(SLOTS):
            copy = pltpu.make_async_copy(*pieces(s, at[SPREAD[s]], at[SPREAD[s]])[n], local.at[s * 5 + n])
            copy.start()
            mine.append((n, copy))
    fetched = []
    for n, (src, dst) in enumerate(((weight, w_buf), (hidden, h_buf), (gates, g_buf))):
        copy = pltpu.make_async_copy(src, dst, local.at[15 + n])
        copy.start()
        fetched.append(copy)

    top[...] = jnp.full(top.shape, LOWEST, jnp.float32)
    acc[...] = jnp.zeros(acc.shape, jnp.float32)

    pl.semaphore_wait(barrier, len(peers))
    exchange((0, 1))
    exchange((2,))

    def exchanged(s, n):
        for step in (1, 3, 2):
            source = shifted(SPREAD[s], RING - step)
            src, dst = pieces(s, at[SPREAD[s]], source)[n]
            remote(src, dst, ex_send.at[s, step, n], ex_recv.at[s, step, n], sibling, start=False).wait_recv()

    def blocks_transposed(block):
        return jnp.concatenate([block[n * HD:(n + 1) * HD].T for n in range(CHUNK // HD)], axis=0)

    def chunk(s, first, second, half=None):
        where = kv.at[s, chip_routed(s, first, second)]
        return where if half is None else where.at[half]

    slot_sends = [0] * SLOTS

    def pass_on(s, first, second, which, step, half=None):
        there = (first - step, second) if which == 0 else (first, second - step)
        there = (there[0] % RING, there[1] % RING)
        ref = chunk(s, first, second, half)
        n = slot_sends[s]
        slot_sends[s] += 1
        remote(
            ref, ref, ag_send.at[s, n],
            ag_recv.at[s, there[0], there[1], 0 if half is None else half],
            routed(s, which, step),
        )
        gathered.append((s, n, first, second, half))

    def arrive(s, first, second):
        across = first if second == 0 else second
        for half in (0, 1) if across == 2 else (None,):
            ref = chunk(s, first, second, half)
            remote(
                ref, ref, ag_send.at[s, 0],
                ag_recv.at[s, first, second, 0 if half is None else half], sibling, start=False,
            ).wait_recv()

    def to_sibling(n, src, dst):
        return remote(src, dst, sib_send.at[n], sib_recv.at[n], sibling, start=False)

    def sibling_queries(s):
        return to_sibling(s, q_in.at[0, s], q_in.at[1, s])

    def partial(s):
        return (
            to_sibling(3 + 2 * s, part.at[0, s], part.at[1, s]),
            to_sibling(4 + 2 * s, level.at[0, s], level.at[1, s]),
        )

    def masked(s, first_column, width):
        row = block_of(lax.broadcasted_iota(jnp.int32, (CHUNK, width), 0))
        column = lax.broadcasted_iota(jnp.int32, (CHUNK, width), 1) + (first_column - CHUNK)
        block = block_of(column)
        if s == 0:
            same = lax.rem(row, 2) == lax.rem(block, 2)
        else:
            same = row == block
        return same & (column >= 0)

    def soften(q, s, cols, scores):
        old = top[q, s, :, cols]
        new = jnp.maximum(old, jnp.max(scores, axis=0, keepdims=True))
        top[q, s, :, cols] = new
        return jnp.exp2(scores - new).astype(jnp.bfloat16), jnp.exp2(old - new)

    def score(q, s, cols, key_block):
        return jnp.dot(
            jnp.concatenate([key_block, key_block], axis=1), qt[q, s, :, cols],
            preferred_element_type=jnp.float32,
        )

    def weigh(q, s, cols, value_blocks, lifted, fade):
        value_block = jnp.concatenate(value_blocks, axis=1)
        ones = jnp.ones((SUMS, value_block.shape[1]), value_block.dtype)
        acc[q, s, :, cols] = acc[q, s, :, cols] * fade + jnp.dot(
            jnp.concatenate([value_block, ones], axis=0), lifted, preferred_element_type=jnp.float32
        )

    def visit(q, chips, masked_slots):
        work = [(s, slice(t, t + TILE)) for s in range(SLOTS) for t in range(0, QUERIES, TILE)]
        scores, lifted = {}, {}
        for j in range(len(work) + 2):
            if j >= 2:
                s, cols = work[j - 2]
                value_blocks = [
                    kv[s, chip, 1, n * HD:(n + 1) * HD, :] for chip in chips[s] for n in range(CHUNK // HD)
                ]
                weigh(q, s, cols, value_blocks, *lifted.pop(j - 2))
            if j < len(work):
                s, cols = work[j]
                key_block = jnp.concatenate([kv[s, chip, 0] for chip in chips[s]], axis=0)
                scores[j] = score(q, s, cols, key_block)
            if 1 <= j <= len(work):
                s, cols = work[j - 1]
                block = scores.pop(j - 1)
                if s in masked_slots and cols.stop > CHUNK:
                    block = jnp.where(masked(s, cols.start, TILE), LOWEST, block)
                lifted[j - 1] = soften(q, s, cols, block)

    def visit_replaced(s, w):
        cols = slice(CHUNK, QUERIES)
        block = score(0, s, cols, kv1[s, w, 0])
        block = jnp.where(masked(s, CHUNK, CHUNK), block, LOWEST)
        value_blocks = [kv1[s, w, 1, n * HD:(n + 1) * HD, :] for n in range(CHUNK // HD)]
        weigh(0, s, cols, value_blocks, *soften(0, s, cols, block))

    def turn_queries(q):
        for s in range(SLOTS):
            for step in range(2):
                for n in range(CHUNK // HD):
                    start = step * CHUNK + n * HD
                    scaled = q_in[q, s, step, n * HD:(n + 1) * HD, :].astype(jnp.float32).T * LOG2_SCALE
                    high = scaled.astype(jnp.bfloat16)
                    qt[q, s, :HD, start:start + HD] = high
                    qt[q, s, HD:, start:start + HD] = (scaled - high.astype(jnp.float32)).astype(jnp.bfloat16)

    for n, copy in mine:
        if n < 2:
            copy.wait()
    for s in range(SLOTS):
        exchanged(s, 0)
        exchanged(s, 1)
        kv[s, own_chip(s), 1] = blocks_transposed(v_in[s])
        for step in (1, 3):
            pass_on(s, 0, 0, 0, step)

    for n, copy in mine:
        if n >= 2:
            copy.wait()
    for s in range(SLOTS):
        exchanged(s, 2)
        sibling_queries(s).start()
    exchange((3, 4))
    turn_queries(0)
    own = [(own_chip(s),) for s in range(SLOTS)]
    visit(0, own, (0, 1, 2))
    for s in range(SLOTS):
        sibling_queries(s).wait_recv()
    turn_queries(1)
    visit(1, own, ())

    def replacement(s, half, hop):
        source = kv1.at[s, 0, half] if hop == 0 else between.at[s, half]
        target = between.at[s, half] if hop == 0 else kv1.at[s, 1, half]
        step = (1, 3)[half]
        return remote(
            source, target, far_send.at[s, half, hop], far_recv.at[s, half, hop],
            device(y=shifted("y", step)), start=False,
        )

    def hand_on():
        for s in range(SLOTS):
            exchanged(s, 3)
            exchanged(s, 4)
            kv1[s, 0, 1] = blocks_transposed(v1_in[s])
            if s > 0:
                for half in range(2):
                    replacement(s, half, 0).start()

    def hand_over():
        for s in (1, 2):
            for half in range(2):
                replacement(s, half, 0).wait_recv()
                replacement(s, half, 1).start()

    def with_partner():
        partner = [(chip_at(s, *PARTNER),) for s in range(SLOTS)]
        visit(1, partner, ())
        visit(0, partner, (1, 2))
        for s in range(SLOTS):
            visit_replaced(s, 0)

    def sibling_done():
        for s in range(SLOTS):
            weight_sum = acc[1, s, HD:HD + 1]
            part[0, s] = (acc[1, s, :HD] / weight_sum).astype(jnp.bfloat16)
            level[0, s] = jnp.broadcast_to(top[1, s] + jnp.log2(weight_sum), level.shape[2:])
            for copy in partial(s):
                copy.start()

    def turn(r, carry):
        for k in range(2 * len(VISITS)):
            if k in ARRIVALS or k in PASSES:
                @pl.when(r == k)
                def _():
                    for s in range(SLOTS):
                        for place in ARRIVALS.get(k, ()):
                            arrive(s, *place)
                    for place, which, step, half in PASSES.get(k, ()):
                        for s in range(SLOTS):
                            pass_on(s, *place, which, step, half)

        pl.when(r == HAND_ON)(hand_on)
        pl.when(r == HAND_ON + 2)(hand_over)
        pl.when(r == WITH_PARTNER)(with_partner)
        pl.when(r == 2 * len(VISITS) - 1)(sibling_done)
        pair = r // 2
        chips = []
        for s in range(SLOTS):
            places = [
                [
                    chip_at(s, *FREE) if place is None else chip_routed(s, *place)
                    for place in (visited[side] for visited in VISITS)
                ]
                for side in range(2)
            ]
            chips.append([
                sum((pair == n).astype(jnp.int32) * place for n, place in enumerate(places[side]))
                for side in range(2)
            ])
        visit(1 - lax.rem(r, 2), chips, ())
        return carry

    lax.fori_loop(0, 2 * len(VISITS), turn, 0)
    for s in (1, 2):
        for half in range(2):
            replacement(s, half, 1).wait_recv()
        visit_replaced(s, 1)

    returns = []
    for s in range(SLOTS):
        axis = SPREAD[s]
        for copy in partial(s):
            copy.wait_recv()
        weight_sum = acc[0, s, HD:HD + 1]
        gap = level[1, s, 0:1] - (top[0, s] + jnp.log2(weight_sum))
        result = (
            acc[0, s, :HD] / (weight_sum * (1.0 + jnp.exp2(gap)))
            + part[1, s].astype(jnp.float32) / (1.0 + jnp.exp2(-gap))
        ).astype(jnp.bfloat16)
        for step in range(2):
            o_out[s, step] = jnp.concatenate(
                [
                    result[:, step * CHUNK + n * HD:step * CHUNK + (n + 1) * HD].T
                    for n in range(CHUNK // HD)
                ],
                axis=0,
            )
        cols = columns_of(4 * s + at[axis])
        for step in (2, 1, 3):
            place = shifted(axis, step)
            sent.append(remote(
                o_out.at[s, :, rows_of(place), :], att.at[:, :, cols],
                ret_send.at[s, step], ret_recv.at[s, step], device(**{axis: place}),
            ))
        copy = pltpu.make_async_copy(o_out.at[s, :, rows_of(at[axis]), :], att.at[:, :, cols], local.at[18 + s])
        copy.start()
        returns.append(copy)
    for copy in fetched + returns:
        copy.wait()
    for s in range(SLOTS):
        axis = SPREAD[s]
        for step in (1, 3, 2):
            source = shifted(axis, RING - step)
            remote(
                o_out.at[s, :, rows_of(at[axis]), :], att.at[:, :, columns_of(4 * s + source)],
                ret_send.at[s, step], ret_recv.at[s, step], sibling, start=False,
            ).wait_recv()

    merged = att[...].reshape(2 * TOK, att.shape[2])
    width = out.shape[2]
    for n in range(0, width, 512):
        cols = slice(n, n + 512)
        projected = jnp.dot(merged, w_buf[:, cols], preferred_element_type=jnp.float32)
        for step in range(2):
            gate = g_buf[pl.ds(steps[step], 1), cols]
            block = projected[step * TOK:(step + 1) * TOK]
            out[step, :, cols] = (h_buf[step, :, cols].astype(jnp.float32) + gate * block).astype(out.dtype)

    for copy in sent:
        copy.wait_send()
    for s in (1, 2):
        for half in range(2):
            for hop in range(2):
                replacement(s, half, hop).wait_send()
    for s in range(SLOTS):
        for copy in (sibling_queries(s),) + partial(s):
            copy.wait_send()
    for s, n, first, second, half in gathered:
        ref = chunk(s, first, second, half)
        remote(ref, ref, ag_send.at[s, n], ag_recv.at[s, 0, 0, 0], sibling, start=False).wait_send()


def shards(hidden, queries, keys, values, out_weight, gate_table, steps_t):
    any_spec = pl.BlockSpec(memory_space=pl.ANY)
    dma = pltpu.SemaphoreType.DMA
    bf16, f32 = jnp.bfloat16, jnp.float32
    return pl.pallas_call(
        kernel,
        out_shape=jax.ShapeDtypeStruct(hidden.shape, hidden.dtype),
        in_specs=[any_spec] * 6 + [pl.BlockSpec(memory_space=pltpu.SMEM)],
        out_specs=pl.BlockSpec(memory_space=pltpu.VMEM),
        scratch_shapes=[
            pltpu.VMEM((SLOTS, RING * RING, 2, CHUNK, HD), bf16),
            pltpu.VMEM((SLOTS, 2, 2, CHUNK, HD), bf16),
            pltpu.VMEM((SLOTS, 2, CHUNK, HD), bf16),
            pltpu.VMEM((SLOTS, CHUNK, HD), bf16),
            pltpu.VMEM((SLOTS, CHUNK, HD), bf16),
            pltpu.VMEM((2, SLOTS, 2, CHUNK, HD), bf16),
            pltpu.VMEM((2, SLOTS, 2 * HD, QUERIES), bf16),
            pltpu.VMEM((2, SLOTS, HD + SUMS, QUERIES), f32),
            pltpu.VMEM((2, SLOTS, 1, QUERIES), f32),
            pltpu.VMEM((2, SLOTS, HD, QUERIES), bf16),
            pltpu.VMEM((2, SLOTS, 8, QUERIES), f32),
            pltpu.VMEM((SLOTS, 2, CHUNK, HD), bf16),
            pltpu.VMEM(queries.shape, bf16),
            pltpu.VMEM(out_weight.shape, bf16),
            pltpu.VMEM(gate_table.shape, f32),
            pltpu.VMEM(hidden.shape, bf16),
            dma((SLOTS, RING, 5)),
            dma((SLOTS, RING, 5)),
            dma((SLOTS, 20)),
            dma((SLOTS, RING, RING, 2)),
            dma((9,)),
            dma((9,)),
            dma((SLOTS, 2, 2)),
            dma((SLOTS, 2, 2)),
            dma((SLOTS, RING)),
            dma((SLOTS, RING)),
            dma((21,)),
        ],
        compiler_params=pltpu.CompilerParams(
            collective_id=0, has_side_effects=True, vmem_limit_bytes=58 * 2**20
        ),
        name="attend",
    )(hidden, queries, keys, values, out_weight, gate_table, steps_t)


def solution(mesh):
    rows = P(None, ("patch", "head"), None)
    return jax.shard_map(
        shards,
        mesh=mesh,
        in_specs=(rows, rows, rows, rows, P(), P(), P()),
        out_specs=rows,
        check_vma=False,
    )
```

```python
import functools
import math

import jax
import jax.numpy as jnp
from jax import lax
from jax.experimental import pallas as pl
from jax.experimental.pallas import tpu as pltpu
from jax.sharding import PartitionSpec as P

HD = 128
TOK = 96
CHUNK = 4 * TOK
QUERIES = 2 * CHUNK
RING = 4
SLOTS = 3
TILE = 256
LOG2_SCALE = math.log2(math.e) / math.sqrt(HD)
LOWEST = -1e30
SUMS = 16

SPREAD = ("y", "x", "z")
PLANE = (("x", "z"), ("y", "z"), ("y", "x"))

VISITS = (
    ((1, 0), (3, 0)), ((0, 1), (0, 3)), ((1, 1), (1, 3)), ((3, 1), (3, 3)),
    ((2, 1), (2, 3)), (None, (1, 2)), ((3, 2), (2, 2)),
)
FREE = (0, 2)
PARTNER = (2, 0)

ARRIVALS = {
    0: ((1, 0), (3, 0)),
    2: ((0, 1), (0, 3)),
    4: ((1, 1), (1, 3)),
    5: ((2, 0),),
    6: ((3, 1), (3, 3)),
    8: ((2, 1), (2, 3)),
    10: ((0, 2), (1, 2)),
    12: ((3, 2), (2, 2)),
}
PASSES = {
    0: (
        ((0, 0), 1, 1, None), ((0, 0), 1, 3, None),
        ((3, 0), 0, 1, 0), ((1, 0), 0, 3, 1),
    ),
    1: (((1, 0), 1, 1, None), ((1, 0), 1, 3, None)),
    3: (((3, 0), 1, 1, None), ((3, 0), 1, 3, None)),
    4: (((0, 3), 1, 1, 0), ((0, 1), 1, 3, 1)),
    5: (((2, 0), 1, 1, None), ((2, 0), 1, 3, None)),
    6: (((1, 3), 1, 1, 0), ((1, 1), 1, 3, 1)),
    7: (((3, 3), 1, 1, 0), ((3, 1), 1, 3, 1)),
    8: (((2, 3), 1, 1, 0), ((2, 1), 1, 3, 1)),
}
HAND_ON = 11
WITH_PARTNER = 11


def block_of(index):
    return sum((index >= edge * TOK).astype(jnp.int32) for edge in range(1, RING))


def kernel(
    hidden, queries, keys, values, weight, gates, steps, out,
    kv, kv1, between, v_in, v1_in, q_in, qt, acc, top, part, level, o_out, att, w_buf, g_buf, h_buf,
    ex_send, ex_recv, ag_send, ag_recv, sib_send, sib_recv, far_send, far_recv, ret_send, ret_recv, local,
):
    patch, head = lax.axis_index("patch"), lax.axis_index("head")
    core = lax.rem(patch, 2)
    at = {
        "x": patch // 16,
        "z": lax.rem(patch // 4, RING),
        "y": head * 2 + lax.rem(patch // 2, 2),
    }

    def device(**moved):
        pos = dict(at, core=core)
        pos.update(moved)
        y = pos["y"]
        return (((pos["x"] * RING + pos["z"]) * 2 + lax.rem(y, 2)) * 2 + pos["core"], y // 2)

    def shifted(axis, step):
        return lax.rem(at[axis] + step, RING)

    def pick(first, second):
        return first + core * (second - first)

    def routed(s, which, step):
        a, b = PLANE[s] if which == 0 else PLANE[s][::-1]
        da, db = device(**{a: shifted(a, step)}), device(**{b: shifted(b, step)})
        return (pick(da[0], db[0]), pick(da[1], db[1]))

    def chip_at(s, da, db):
        a, b = PLANE[s]
        return shifted(a, da) * RING + shifted(b, db)

    def chip_routed(s, first, second):
        return pick(chip_at(s, first, second), chip_at(s, second, first))

    sibling = device(core=1 - core)

    peers = [device(**{axis: shifted(axis, step)}) for axis in "xyz" for step in (1, 2, 3)]
    peers.append(sibling)
    barrier = pltpu.get_barrier_semaphore()
    for peer in peers:
        pl.semaphore_signal(barrier, inc=1, device_id=peer, device_id_type=pl.DeviceIdType.MESH)

    sent, gathered = [], []

    def remote(src, dst, send_sem, recv_sem, target, start=True):
        copy = pltpu.make_async_remote_copy(
            src_ref=src, dst_ref=dst, send_sem=send_sem, recv_sem=recv_sem,
            device_id=target, device_id_type=pl.DeviceIdType.MESH,
        )
        if start:
            copy.start()
        return copy

    def rows_of(place):
        return pl.ds(pl.multiple_of(place * TOK, TOK), TOK)

    def columns_of(place):
        return pl.ds(pl.multiple_of(place * HD, HD), HD)

    def own_chip(s):
        return chip_at(s, 0, 0)

    def pieces(s, target_place, source_place):
        cols = columns_of(4 * s + target_place)
        rows = rows_of(source_place)
        return (
            (keys.at[0, :, cols], kv.at[s, own_chip(s), 0, rows, :]),
            (values.at[0, :, cols], v_in.at[s, rows, :]),
            (queries.at[:, :, cols], q_in.at[0, s, :, rows, :]),
            (keys.at[1, :, cols], kv1.at[s, 0, 0, rows, :]),
            (values.at[1, :, cols], v1_in.at[s, rows, :]),
        )

    def exchange(group):
        for step in (1, 3, 2):
            for s in range(SLOTS):
                axis = SPREAD[s]
                place = shifted(axis, step)
                both = pieces(s, place, at[axis])
                for n in group:
                    sent.append(remote(
                        *both[n], ex_send.at[s, step, n], ex_recv.at[s, step, n], device(**{axis: place})
                    ))

    mine = []
    for n in range(5):
        for s in range(SLOTS):
            copy = pltpu.make_async_copy(*pieces(s, at[SPREAD[s]], at[SPREAD[s]])[n], local.at[s * 5 + n])
            copy.start()
            mine.append((n, copy))
    fetched = []
    for n, (src, dst) in enumerate(((weight, w_buf), (hidden, h_buf), (gates, g_buf))):
        copy = pltpu.make_async_copy(src, dst, local.at[15 + n])
        copy.start()
        fetched.append(copy)

    top[...] = jnp.full(top.shape, LOWEST, jnp.float32)
    acc[...] = jnp.zeros(acc.shape, jnp.float32)

    pl.semaphore_wait(barrier, len(peers))
    exchange((0, 1))
    exchange((2,))

    def exchanged(s, n):
        for step in (1, 3, 2):
            source = shifted(SPREAD[s], RING - step)
            src, dst = pieces(s, at[SPREAD[s]], source)[n]
            remote(src, dst, ex_send.at[s, step, n], ex_recv.at[s, step, n], sibling, start=False).wait_recv()

    def blocks_transposed(block):
        return jnp.concatenate([block[n * HD:(n + 1) * HD].T for n in range(CHUNK // HD)], axis=0)

    def chunk(s, first, second, half=None):
        where = kv.at[s, chip_routed(s, first, second)]
        return where if half is None else where.at[half]

    slot_sends = [0] * SLOTS

    def pass_on(s, first, second, which, step, half=None):
        there = (first - step, second) if which == 0 else (first, second - step)
        there = (there[0] % RING, there[1] % RING)
        ref = chunk(s, first, second, half)
        n = slot_sends[s]
        slot_sends[s] += 1
        remote(
            ref, ref, ag_send.at[s, n],
            ag_recv.at[s, there[0], there[1], 0 if half is None else half],
            routed(s, which, step),
        )
        gathered.append((s, n, first, second, half))

    def arrive(s, first, second):
        across = first if second == 0 else second
        for half in (0, 1) if across == 2 else (None,):
            ref = chunk(s, first, second, half)
            remote(
                ref, ref, ag_send.at[s, 0],
                ag_recv.at[s, first, second, 0 if half is None else half], sibling, start=False,
            ).wait_recv()

    def to_sibling(n, src, dst):
        return remote(src, dst, sib_send.at[n], sib_recv.at[n], sibling, start=False)

    def sibling_queries(s):
        return to_sibling(s, q_in.at[0, s], q_in.at[1, s])

    def partial(s):
        return (
            to_sibling(3 + 2 * s, part.at[0, s], part.at[1, s]),
            to_sibling(4 + 2 * s, level.at[0, s], level.at[1, s]),
        )

    def masked(s, first_column, width):
        row = block_of(lax.broadcasted_iota(jnp.int32, (CHUNK, width), 0))
        column = lax.broadcasted_iota(jnp.int32, (CHUNK, width), 1) + (first_column - CHUNK)
        block = block_of(column)
        if s == 0:
            same = lax.rem(row, 2) == lax.rem(block, 2)
        else:
            same = row == block
        return same & (column >= 0)

    def soften(q, s, cols, scores):
        old = top[q, s, :, cols]
        new = jnp.maximum(old, jnp.max(scores, axis=0, keepdims=True))
        top[q, s, :, cols] = new
        return jnp.exp2(scores - new).astype(jnp.bfloat16), jnp.exp2(old - new)

    def score(q, s, cols, key_block):
        return jnp.dot(
            jnp.concatenate([key_block, key_block], axis=1), qt[q, s, :, cols],
            preferred_element_type=jnp.float32,
        )

    def weigh(q, s, cols, value_blocks, lifted, fade):
        value_block = jnp.concatenate(value_blocks, axis=1)
        ones = jnp.ones((SUMS, value_block.shape[1]), value_block.dtype)
        acc[q, s, :, cols] = acc[q, s, :, cols] * fade + jnp.dot(
            jnp.concatenate([value_block, ones], axis=0), lifted, preferred_element_type=jnp.float32
        )

    def visit(q, chips, masked_slots):
        work = [(s, slice(t, t + TILE)) for s in range(SLOTS) for t in range(0, QUERIES, TILE)]
        scores, lifted = {}, {}
        for j in range(len(work) + 2):
            if j >= 2:
                s, cols = work[j - 2]
                value_blocks = [
                    kv[s, chip, 1, n * HD:(n + 1) * HD, :] for chip in chips[s] for n in range(CHUNK // HD)
                ]
                weigh(q, s, cols, value_blocks, *lifted.pop(j - 2))
            if j < len(work):
                s, cols = work[j]
                key_block = jnp.concatenate([kv[s, chip, 0] for chip in chips[s]], axis=0)
                scores[j] = score(q, s, cols, key_block)
            if 1 <= j <= len(work):
                s, cols = work[j - 1]
                block = scores.pop(j - 1)
                if s in masked_slots and cols.stop > CHUNK:
                    block = jnp.where(masked(s, cols.start, TILE), LOWEST, block)
                lifted[j - 1] = soften(q, s, cols, block)

    def visit_replaced(s, w):
        cols = slice(CHUNK, QUERIES)
        block = score(0, s, cols, kv1[s, w, 0])
        block = jnp.where(masked(s, CHUNK, CHUNK), block, LOWEST)
        value_blocks = [kv1[s, w, 1, n * HD:(n + 1) * HD, :] for n in range(CHUNK // HD)]
        weigh(0, s, cols, value_blocks, *soften(0, s, cols, block))

    def turn_queries(q):
        for s in range(SLOTS):
            for step in range(2):
                for n in range(CHUNK // HD):
                    start = step * CHUNK + n * HD
                    scaled = q_in[q, s, step, n * HD:(n + 1) * HD, :].T.astype(jnp.float32) * LOG2_SCALE
                    high = scaled.astype(jnp.bfloat16)
                    qt[q, s, :HD, start:start + HD] = high
                    qt[q, s, HD:, start:start + HD] = (scaled - high.astype(jnp.float32)).astype(jnp.bfloat16)

    for n, copy in mine:
        if n < 2:
            copy.wait()
    for s in range(SLOTS):
        exchanged(s, 0)
        exchanged(s, 1)
        kv[s, own_chip(s), 1] = blocks_transposed(v_in[s])
        for step in (1, 3):
            pass_on(s, 0, 0, 0, step)

    for n, copy in mine:
        if n >= 2:
            copy.wait()
    for s in range(SLOTS):
        exchanged(s, 2)
        sibling_queries(s).start()
    exchange((3, 4))
    turn_queries(0)
    own = [(own_chip(s),) for s in range(SLOTS)]
    visit(0, own, (0, 1, 2))
    for s in range(SLOTS):
        sibling_queries(s).wait_recv()
    turn_queries(1)
    visit(1, own, ())

    def replacement(s, half, hop):
        source = kv1.at[s, 0, half] if hop == 0 else between.at[s, half]
        target = between.at[s, half] if hop == 0 else kv1.at[s, 1, half]
        step = (1, 3)[half]
        return remote(
            source, target, far_send.at[s, half, hop], far_recv.at[s, half, hop],
            device(y=shifted("y", step)), start=False,
        )

    def hand_on():
        for s in range(SLOTS):
            exchanged(s, 3)
            exchanged(s, 4)
            kv1[s, 0, 1] = blocks_transposed(v1_in[s])
            if s > 0:
                for half in range(2):
                    replacement(s, half, 0).start()

    def hand_over():
        for s in (1, 2):
            for half in range(2):
                replacement(s, half, 0).wait_recv()
                replacement(s, half, 1).start()

    def with_partner():
        partner = [(chip_at(s, *PARTNER),) for s in range(SLOTS)]
        visit(1, partner, ())
        visit(0, partner, (1, 2))
        for s in range(SLOTS):
            visit_replaced(s, 0)

    def sibling_done():
        for s in range(SLOTS):
            weight_sum = acc[1, s, HD:HD + 1]
            part[0, s] = (acc[1, s, :HD] / weight_sum).astype(jnp.bfloat16)
            level[0, s] = jnp.broadcast_to(top[1, s] + jnp.log2(weight_sum), level.shape[2:])
            for copy in partial(s):
                copy.start()

    def turn(r, carry):
        for k in range(2 * len(VISITS)):
            if k in ARRIVALS or k in PASSES:
                @pl.when(r == k)
                def _():
                    for s in range(SLOTS):
                        for place in ARRIVALS.get(k, ()):
                            arrive(s, *place)
                    for place, which, step, half in PASSES.get(k, ()):
                        for s in range(SLOTS):
                            pass_on(s, *place, which, step, half)

        pl.when(r == HAND_ON)(hand_on)
        pl.when(r == HAND_ON + 2)(hand_over)
        pl.when(r == WITH_PARTNER)(with_partner)
        pl.when(r == 2 * len(VISITS) - 1)(sibling_done)
        pair = r // 2
        chips = []
        for s in range(SLOTS):
            places = [
                [
                    chip_at(s, *FREE) if place is None else chip_routed(s, *place)
                    for place in (visited[side] for visited in VISITS)
                ]
                for side in range(2)
            ]
            chips.append([
                sum((pair == n).astype(jnp.int32) * place for n, place in enumerate(places[side]))
                for side in range(2)
            ])
        visit(1 - lax.rem(r, 2), chips, ())
        return carry

    lax.fori_loop(0, 2 * len(VISITS), turn, 0)
    for s in (1, 2):
        for half in range(2):
            replacement(s, half, 1).wait_recv()
        visit_replaced(s, 1)

    returns = []
    for s in range(SLOTS):
        axis = SPREAD[s]
        for copy in partial(s):
            copy.wait_recv()
        weight_sum = acc[0, s, HD:HD + 1]
        gap = level[1, s, 0:1] - (top[0, s] + jnp.log2(weight_sum))
        result = (
            acc[0, s, :HD] / (weight_sum * (1.0 + jnp.exp2(gap)))
            + part[1, s].astype(jnp.float32) / (1.0 + jnp.exp2(-gap))
        ).astype(jnp.bfloat16)
        for step in range(2):
            o_out[s, step] = jnp.concatenate(
                [
                    result[:, step * CHUNK + n * HD:step * CHUNK + (n + 1) * HD].T
                    for n in range(CHUNK // HD)
                ],
                axis=0,
            )
        cols = columns_of(4 * s + at[axis])
        for step in (2, 1, 3):
            place = shifted(axis, step)
            sent.append(remote(
                o_out.at[s, :, rows_of(place), :], att.at[:, :, cols],
                ret_send.at[s, step], ret_recv.at[s, step], device(**{axis: place}),
            ))
        copy = pltpu.make_async_copy(o_out.at[s, :, rows_of(at[axis]), :], att.at[:, :, cols], local.at[18 + s])
        copy.start()
        returns.append(copy)
    for copy in fetched + returns:
        copy.wait()
    for s in range(SLOTS):
        axis = SPREAD[s]
        for step in (1, 3, 2):
            source = shifted(axis, RING - step)
            remote(
                o_out.at[s, :, rows_of(at[axis]), :], att.at[:, :, columns_of(4 * s + source)],
                ret_send.at[s, step], ret_recv.at[s, step], sibling, start=False,
            ).wait_recv()

    merged = att[...].reshape(2 * TOK, att.shape[2])
    width = out.shape[2]
    for n in range(0, width, 512):
        cols = slice(n, n + 512)
        projected = jnp.dot(merged, w_buf[:, cols], preferred_element_type=jnp.float32)
        for step in range(2):
            gate = g_buf[pl.ds(steps[step], 1), cols]
            block = projected[step * TOK:(step + 1) * TOK]
            out[step, :, cols] = (h_buf[step, :, cols].astype(jnp.float32) + gate * block).astype(out.dtype)

    for copy in sent:
        copy.wait_send()
    for s in (1, 2):
        for half in range(2):
            for hop in range(2):
                replacement(s, half, hop).wait_send()
    for s in range(SLOTS):
        for copy in (sibling_queries(s),) + partial(s):
            copy.wait_send()
    for s, n, first, second, half in gathered:
        ref = chunk(s, first, second, half)
        remote(ref, ref, ag_send.at[s, n], ag_recv.at[s, 0, 0, 0], sibling, start=False).wait_send()


def shards(hidden, queries, keys, values, out_weight, gate_table, steps_t):
    any_spec = pl.BlockSpec(memory_space=pl.ANY)
    dma = pltpu.SemaphoreType.DMA
    bf16, f32 = jnp.bfloat16, jnp.float32
    return pl.pallas_call(
        kernel,
        out_shape=jax.ShapeDtypeStruct(hidden.shape, hidden.dtype),
        in_specs=[any_spec] * 6 + [pl.BlockSpec(memory_space=pltpu.SMEM)],
        out_specs=pl.BlockSpec(memory_space=pltpu.VMEM),
        scratch_shapes=[
            pltpu.VMEM((SLOTS, RING * RING, 2, CHUNK, HD), bf16),
            pltpu.VMEM((SLOTS, 2, 2, CHUNK, HD), bf16),
            pltpu.VMEM((SLOTS, 2, CHUNK, HD), bf16),
            pltpu.VMEM((SLOTS, CHUNK, HD), bf16),
            pltpu.VMEM((SLOTS, CHUNK, HD), bf16),
            pltpu.VMEM((2, SLOTS, 2, CHUNK, HD), bf16),
            pltpu.VMEM((2, SLOTS, 2 * HD, QUERIES), bf16),
            pltpu.VMEM((2, SLOTS, HD + SUMS, QUERIES), f32),
            pltpu.VMEM((2, SLOTS, 1, QUERIES), f32),
            pltpu.VMEM((2, SLOTS, HD, QUERIES), bf16),
            pltpu.VMEM((2, SLOTS, 8, QUERIES), f32),
            pltpu.VMEM((SLOTS, 2, CHUNK, HD), bf16),
            pltpu.VMEM(queries.shape, bf16),
            pltpu.VMEM(out_weight.shape, bf16),
            pltpu.VMEM(gate_table.shape, f32),
            pltpu.VMEM(hidden.shape, bf16),
            dma((SLOTS, RING, 5)),
            dma((SLOTS, RING, 5)),
            dma((SLOTS, 20)),
            dma((SLOTS, RING, RING, 2)),
            dma((9,)),
            dma((9,)),
            dma((SLOTS, 2, 2)),
            dma((SLOTS, 2, 2)),
            dma((SLOTS, RING)),
            dma((SLOTS, RING)),
            dma((21,)),
        ],
        compiler_params=pltpu.CompilerParams(
            collective_id=0, has_side_effects=True, vmem_limit_bytes=58 * 2**20
        ),
        name="attend",
    )(hidden, queries, keys, values, out_weight, gate_table, steps_t)


def solution(mesh):
    rows = P(None, ("patch", "head"), None)
    return jax.shard_map(
        shards,
        mesh=mesh,
        in_specs=(rows, rows, rows, rows, P(), P(), P()),
        out_specs=rows,
        check_vma=False,
    )
```
